32 devices in a mesh: grp: 4 (over x, core), cell: 8 (over z, y).
Axes of the slice: x: 2, y: 2, z: 4, core: 2. Of those that a mesh axis runs over, the one named last changes fastest.
Arguments:
- rhs: float32 [64, 2, 32, 16, 128], P('grp', None, 'cell'), may hold values from -8 to 8
- log_perm: float32 [64, 32, 16, 128], P('grp', 'cell'), may hold values from -1.5 to 1.5
- porosity: float32 [64, 32, 16, 128], P('grp', 'cell'), may hold values from 0.1 to 0.3
- saturation: float32 [64, 32, 16, 128], P('grp', 'cell'), may hold values from 0.2 to 0.8
- pressure: float32 [64, 32, 16, 128], P('grp', 'cell'), may hold values from -6 to 6
- obs_values: float32 [256], replicated, may hold values from -6 to 6
- obs_error: float32 [256], replicated, may hold values from 0.1 to 1
- noise: float32 [64, 256], replicated, may hold values from -6 to 6
- well_cell: int32 [128], replicated, may hold values from 0 to 65535
- obs_well: int32 [256], replicated, may hold values from 0 to 127
Outputs:
- increment: float32 [64, 2, 32, 16, 128], P('grp', None, 'cell')
- log_perm_post: float32 [64, 32, 16, 128], P('grp', 'cell')
- porosity_post: float32 [64, 32, 16, 128], P('grp', 'cell')
The draws below stay inside these ranges and needn't reach their ends.
All inputs are finite; a program needn't handle non-finite values.
Results may differ from the reference program's by a relative error of at most 0.0003.
Values sent between devices are 32-bit elements; how exact they have to be, the bound alone decides.
A program may use at most 128 MiB of HBM per device.

```python
import math
import jax
import jax.numpy as jnp
from jax import lax

NY = 16
NZ = 128
KRYLOV = 4
NWELL = 128
NOBS = 256
MEMBERS = 64
NX = 32


def draw_rhs(key, part):
    shape = (MEMBERS, 2, NX, NY, NZ)
    position = jnp.arange(NX, dtype=jnp.float32) / max(NX - 1, 1)
    ramp = (1.0 + 2.0 * position)[None, None, :, None, None]
    values = jax.random.normal(key, shape, jnp.float32) * ramp
    return jnp.clip(values, -8.0, 8.0)


def with_ends(values, own_key, smallest, largest):
    longest = values.shape.index(max(values.shape))
    spots = []
    for shift in (0, 1):
        where = [jax.random.randint(jax.random.fold_in(own_key, axis), (), 0, length) for axis, length in enumerate(values.shape)]
        where[longest] = (where[longest] + shift) % values.shape[longest]
        spots.append(tuple(where))
    return values.at[spots[0]].set(smallest).at[spots[1]].set(largest)


def block_levels(own_key, extent, pieces, smallest, largest):
    factor_of, own = 1.0, jax.random.fold_in(own_key, 6)
    for axis_at, shards_of in pieces:
        steps = jnp.exp(jax.random.uniform(jax.random.fold_in(own, axis_at), (shards_of,), jnp.float32, smallest / len(pieces), largest / len(pieces)))
        factor_of = factor_of * jnp.repeat(steps, extent[axis_at] // shards_of).reshape([-1 if axis == axis_at else 1 for axis in range(len(extent))])
    return factor_of


def normal_values(own_key, extent, width, reach, split=(), held_as=jnp.bfloat16):
    factor_of = block_levels(own_key, extent, split, -0.22, 0.18) if split else 1.0
    drawn = jax.random.normal(own_key, extent, jnp.float32) * width * factor_of
    return jnp.minimum(jnp.maximum(drawn, -reach), reach).astype(held_as)


def setup_inputs(seed: int = 0) -> dict:
    keys = jax.random.split(jax.random.key(seed), 11)
    return {
        "rhs": draw_rhs(jax.random.fold_in(keys[10], 71), 0),
        "log_perm": jnp.clip(jax.random.uniform(keys[1], (MEMBERS, NX, NY, NZ), jnp.float32, -1.5, 1.5) * block_levels(keys[1], (MEMBERS, NX, NY, NZ), ((0, 4), (1, 8)), -0.4, 0.0), -1.5, 1.5),
        "porosity": jnp.clip(0.1 + 0.20000001043081284 * jax.random.uniform(keys[2], (MEMBERS, NX, NY, NZ), jnp.float32) ** block_levels(keys[2], (MEMBERS, NX, NY, NZ), ((0, 4), (1, 8)), -0.2, 0.2), 0.1, 0.3),
        "saturation": jnp.clip(0.2 + 0.6 * jax.random.uniform(keys[3], (MEMBERS, NX, NY, NZ), jnp.float32) ** block_levels(keys[3], (MEMBERS, NX, NY, NZ), ((0, 4), (1, 8)), -0.2, 0.2), 0.2, 0.8),
        "pressure": normal_values(keys[4], (MEMBERS, NX, NY, NZ), 1.0, 6.0, ((0, 4), (1, 8)), jnp.float32),
        "obs_values": normal_values(keys[5], (NOBS,), 1.0, 6.0, (), jnp.float32),
        "obs_error": jnp.clip(jnp.exp(jax.random.uniform(keys[6], (NOBS,), jnp.float32, math.log(0.1), math.log(1.0))), 0.1, 1.0),
        "noise": normal_values(keys[7], (MEMBERS, NOBS), 1.0, 6.0, (), jnp.float32),
        "well_cell": with_ends(jax.random.randint(keys[8], (NWELL,), 0, NX * NY * NZ), jax.random.fold_in(keys[8], 1), 0, (NX * NY * NZ) - 1).astype(jnp.int32),
        "obs_well": with_ends(jax.random.randint(keys[9], (NOBS,), 0, NWELL), jax.random.fold_in(keys[9], 1), 0, NWELL - 1).astype(jnp.int32),
    }


epsilon = 1e-06
time_step = 0.1
compress = 0.5
inflation = 4.0

def mobility(sat_field):
    return sat_field * sat_field + 0.5 * (1.0 - sat_field) * (1.0 - sat_field)

def face_pair(perm_low, perm_high, sat_low, sat_high):
    trans = 2.0 * perm_low * perm_high / (perm_low + perm_high) * (0.5 * (mobility(sat_low) + mobility(sat_high)))
    return (trans, trans * (0.5 * (sat_low + sat_high)))

def plane_faces(perm, sat_field):
    plane_rows = perm.shape[-2]
    plane_cols = perm.shape[-1]
    keep_rows = (lax.broadcasted_iota(jnp.int32, (plane_rows, plane_cols), 0) < plane_rows - 1).astype(jnp.float32)
    keep_cols = (lax.broadcasted_iota(jnp.int32, (plane_rows, plane_cols), 1) < plane_cols - 1).astype(jnp.float32)
    trans_y, frac_y = face_pair(perm, jnp.roll(perm, -1, -2), sat_field, jnp.roll(sat_field, -1, -2))
    trans_z, frac_z = face_pair(perm, jnp.roll(perm, -1, -1), sat_field, jnp.roll(sat_field, -1, -1))
    return (trans_y * keep_rows, frac_y * keep_rows, trans_z * keep_cols, frac_z * keep_cols)

def operator(padded, second, coeffs):
    accum, trans_x, frac_x, trans_y, frac_y, trans_z, frac_z = coeffs
    first = padded[..., 1:-1, :, :]
    diff_x = padded[..., 1:, :, :] - padded[..., :-1, :, :]
    diff_y = jnp.roll(first, -1, -2) - first
    diff_z = jnp.roll(first, -1, -1) - first

    def net(coef_x, coef_y, coef_z):
        flow_x = coef_x * diff_x
        flow_y = coef_y * diff_y
        flow_z = coef_z * diff_z
        return flow_x[..., :-1, :, :] - flow_x[..., 1:, :, :] + (jnp.roll(flow_y, 1, -2) - flow_y) + (jnp.roll(flow_z, 1, -1) - flow_z)
    out_pressure = accum * (compress * first + 0.5 * second) + net(trans_x, trans_y, trans_z)
    out_water = accum * second + net(frac_x, frac_y, frac_z)
    return (out_pressure, out_water)

def least_squares(columns, beta):
    rows = [list(column) for column in columns]
    cosines = []
    sines = []
    target = [beta] + [jnp.zeros_like(beta) for column in columns]
    for jdx in range(len(rows)):
        column = rows[jdx]
        for idx in range(jdx):
            upper = cosines[idx] * column[idx] + sines[idx] * column[idx + 1]
            column[idx + 1] = -sines[idx] * column[idx] + cosines[idx] * column[idx + 1]
            column[idx] = upper
        radius = jnp.sqrt(column[jdx] * column[jdx] + column[jdx + 1] * column[jdx + 1])
        cosines.append(column[jdx] / radius)
        sines.append(column[jdx + 1] / radius)
        column[jdx] = radius
        target[jdx + 1] = -sines[jdx] * target[jdx]
        target[jdx] = cosines[jdx] * target[jdx]
    count = len(rows)
    solved = [None] * count
    for jdx in reversed(range(count)):
        partial_sum = target[jdx]
        for idx in range(jdx + 1, count):
            partial_sum = partial_sum - rows[idx][jdx] * solved[idx]
        solved[jdx] = partial_sum / rows[jdx][jdx]
    return solved

def member_coeffs(lperm, sat_field, poro):
    perm = jnp.exp(lperm)
    trans_x, frac_x = face_pair(perm[:-1], perm[1:], sat_field[:-1], sat_field[1:])
    trans_x = jnp.pad(trans_x, ((1, 1), (0, 0), (0, 0)))
    frac_x = jnp.pad(frac_x, ((1, 1), (0, 0), (0, 0)))
    trans_y, frac_y, trans_z, frac_z = plane_faces(perm, sat_field)
    return (poro / time_step, trans_x, frac_x, trans_y, frac_y, trans_z, frac_z)

def solve_member(inputs):
    rhs_member, lperm, sat_field, poro = inputs
    coeffs = member_coeffs(lperm, sat_field, poro)

    def inner(left, right):
        return jnp.sum(left * right)

    def apply(vector):
        padded = jnp.pad(vector[0], ((1, 1), (0, 0), (0, 0)))
        out_pressure, out_water = operator(padded, vector[1], coeffs)
        return jnp.stack([out_pressure, out_water], 0)
    beta = jnp.sqrt(inner(rhs_member, rhs_member) + epsilon)
    basis = [rhs_member / beta]
    columns = []
    for jdx in range(KRYLOV):
        image = apply(basis[jdx])
        projected = [inner(basis[idx], image) for idx in range(jdx + 1)]
        for idx in range(jdx + 1):
            image = image - projected[idx] * basis[idx]
        height = jnp.sqrt(inner(image, image) + epsilon)
        columns.append(projected + [height])
        basis.append(image / height)
    solved = least_squares(columns, beta)
    result = solved[0] * basis[0]
    for jdx in range(1, KRYLOV):
        result = result + solved[jdx] * basis[jdx]
    return result

def ensemble_weights(predicted, obs_values, obs_error, noise):
    members = predicted.shape[0]
    sigma = math.sqrt(inflation) * obs_error
    center = lax.optimization_barrier(jnp.mean(predicted, axis=0))
    spread = (predicted - center) / (math.sqrt(members - 1.0) * sigma)
    innov = (obs_values + sigma * noise - predicted) / sigma
    gram = jnp.eye(members, dtype=jnp.float32) + jnp.dot(spread.astype(jnp.float32), spread.T.astype(jnp.float32), precision=lax.Precision.HIGHEST, preferred_element_type=jnp.float32)
    cross = jnp.dot(spread.astype(jnp.float32), innov.T.astype(jnp.float32), precision=lax.Precision.HIGHEST, preferred_element_type=jnp.float32)
    factor = jnp.linalg.cholesky(gram)
    return jax.scipy.linalg.cho_solve((factor, True), cross)

def reference(rhs, log_perm, porosity, saturation, pressure, obs_values, obs_error, noise, well_cell, obs_well):
    increment = lax.map(solve_member, (rhs, log_perm, saturation, porosity))
    cells_all = NX * NY * NZ
    flat = jnp.stack([pressure + increment[:, 0], saturation + increment[:, 1]], 1).reshape(MEMBERS, 2 * cells_all)
    cells = jnp.take(well_cell, obs_well).astype(jnp.int32)
    component = (jnp.arange(NOBS, dtype=jnp.int32) >= NWELL).astype(jnp.int32)
    predicted = jnp.take(flat, component * cells_all + cells, axis=1)
    weights = ensemble_weights(predicted, obs_values, obs_error, noise)
    params = jnp.stack([log_perm, porosity], 1).reshape(MEMBERS, 2 * cells_all)
    scaled = params / math.sqrt(MEMBERS - 1.0)
    update = jnp.dot(weights.T.astype(jnp.float32), scaled.astype(jnp.float32), precision=lax.Precision.HIGHEST, preferred_element_type=jnp.float32)
    posterior = (params + update).reshape(MEMBERS, 2, NX, NY, NZ)
    return (increment, posterior[:, 0], posterior[:, 1])
```

```python
import math

import jax
import jax.numpy as jnp
from jax import lax
from jax.sharding import PartitionSpec as P

KRYLOV = 4


epsilon = 1e-06
time_step = 0.1
compress = 0.5
inflation = 4.0


def with_halo(block, sides, width):
    for axis, dim in sides:
        count = lax.axis_size(axis)
        forward = [(i, i + 1) for i in range(count - 1)]
        backward = [(target, source) for source, target in forward]
        low = lax.ppermute(
            lax.slice_in_dim(block, block.shape[dim] - width, None, axis=dim), axis, forward
        )
        high = lax.ppermute(lax.slice_in_dim(block, 0, width, axis=dim), axis, backward)
        block = jnp.concatenate([low, block, high], axis=dim)
    return block


def mobility(sat_field):
    return sat_field * sat_field + 0.5 * (1.0 - sat_field) * (1.0 - sat_field)


def face_pair(perm_low, perm_high, sat_low, sat_high):
    trans = (
        2.0
        * perm_low
        * perm_high
        / (perm_low + perm_high)
        * (0.5 * (mobility(sat_low) + mobility(sat_high)))
    )
    return (trans, trans * (0.5 * (sat_low + sat_high)))


def plane_faces(perm, sat_field):
    plane_rows = perm.shape[-2]
    plane_cols = perm.shape[-1]
    keep_rows = (
        lax.broadcasted_iota(jnp.int32, (plane_rows, plane_cols), 0) < plane_rows - 1
    ).astype(jnp.float32)
    keep_cols = (
        lax.broadcasted_iota(jnp.int32, (plane_rows, plane_cols), 1) < plane_cols - 1
    ).astype(jnp.float32)
    trans_y, frac_y = face_pair(
        perm, jnp.roll(perm, -1, -2), sat_field, jnp.roll(sat_field, -1, -2)
    )
    trans_z, frac_z = face_pair(
        perm, jnp.roll(perm, -1, -1), sat_field, jnp.roll(sat_field, -1, -1)
    )
    return (trans_y * keep_rows, frac_y * keep_rows, trans_z * keep_cols, frac_z * keep_cols)


def operator(padded, second, coeffs):
    accum, trans_x, frac_x, trans_y, frac_y, trans_z, frac_z = coeffs
    first = padded[..., 1:-1, :, :]
    diff_x = padded[..., 1:, :, :] - padded[..., :-1, :, :]
    diff_y = jnp.roll(first, -1, -2) - first
    diff_z = jnp.roll(first, -1, -1) - first

    def net(coef_x, coef_y, coef_z):
        flow_x = coef_x * diff_x
        flow_y = coef_y * diff_y
        flow_z = coef_z * diff_z
        return (
            flow_x[..., :-1, :, :]
            - flow_x[..., 1:, :, :]
            + (jnp.roll(flow_y, 1, -2) - flow_y)
            + (jnp.roll(flow_z, 1, -1) - flow_z)
        )

    out_pressure = accum * (compress * first + 0.5 * second) + net(trans_x, trans_y, trans_z)
    out_water = accum * second + net(frac_x, frac_y, frac_z)
    return (out_pressure, out_water)


def least_squares(columns, beta):
    rows = [list(column) for column in columns]
    cosines = []
    sines = []
    target = [beta] + [jnp.zeros_like(beta) for column in columns]
    for jdx in range(len(rows)):
        column = rows[jdx]
        for idx in range(jdx):
            upper = cosines[idx] * column[idx] + sines[idx] * column[idx + 1]
            column[idx + 1] = -sines[idx] * column[idx] + cosines[idx] * column[idx + 1]
            column[idx] = upper
        radius = jnp.sqrt(column[jdx] * column[jdx] + column[jdx + 1] * column[jdx + 1])
        cosines.append(column[jdx] / radius)
        sines.append(column[jdx + 1] / radius)
        column[jdx] = radius
        target[jdx + 1] = -sines[jdx] * target[jdx]
        target[jdx] = cosines[jdx] * target[jdx]
    count = len(rows)
    solved = [None] * count
    for jdx in reversed(range(count)):
        partial_sum = target[jdx]
        for idx in range(jdx + 1, count):
            partial_sum = partial_sum - rows[idx][jdx] * solved[idx]
        solved[jdx] = partial_sum / rows[jdx][jdx]
    return solved


SHIFTS = (2.0, 7.0, 4.5, 1.0)


def krylov_coefficients(entries):
    size = KRYLOV + 1
    zero = jnp.zeros_like(entries[0])

    def gram(row, col):
        row, col = max(row, col), min(row, col)
        return entries[row * (row + 1) // 2 + col]

    def times_gram(coef):
        out = []
        for row in range(size):
            total = zero
            for col, value in enumerate(coef):
                if value is not None:
                    total = total + gram(row, col) * value
            out.append(total)
        return out

    def dot(coef, image):
        total = zero
        for value, other in zip(coef, image):
            if value is not None:
                total = total + value * other
        return total

    beta = jnp.sqrt(gram(0, 0) + epsilon)
    basis = [[1.0 / beta] + [None] * KRYLOV]
    columns = []
    for jdx in range(KRYLOV):
        image = [None] * size
        for idx in range(jdx + 1):
            value = basis[jdx][idx]
            base = SHIFTS[idx] * value
            image[idx] = base if image[idx] is None else image[idx] + base
            image[idx + 1] = value
        mapped = times_gram(image)
        projected = [dot(basis[idx], mapped) for idx in range(jdx + 1)]
        for idx in range(jdx + 1):
            for pos in range(idx + 1):
                image[pos] = image[pos] - projected[idx] * basis[idx][pos]
        height = jnp.sqrt(jnp.maximum(dot(image, times_gram(image)), 0.0) + epsilon)
        columns.append(projected + [height])
        basis.append([None if value is None else value / height for value in image])
    solved = least_squares(columns, beta)
    mixed = []
    for pos in range(KRYLOV):
        total = zero
        for jdx in range(pos, KRYLOV):
            total = total + solved[jdx] * basis[jdx][pos]
        mixed.append(total)
    return mixed


def ensemble_weights(predicted, obs_values, obs_error, noise):
    members = predicted.shape[0]
    sigma = math.sqrt(inflation) * obs_error
    center = jnp.mean(predicted, axis=0)
    spread = (predicted - center) / (math.sqrt(members - 1.0) * sigma)
    innov = (obs_values + sigma * noise - predicted) / sigma
    gram = jnp.eye(members, dtype=jnp.float32) + jnp.dot(
        spread, spread.T, precision=lax.Precision.HIGHEST, preferred_element_type=jnp.float32
    )
    cross = jnp.dot(
        spread, innov.T, precision=lax.Precision.HIGHEST, preferred_element_type=jnp.float32
    )
    factor = jnp.linalg.cholesky(gram)
    return jax.scipy.linalg.cho_solve((factor, True), cross)


def expand(values):
    return values[:, None, None, None, None]


def inner(left, right):
    return jnp.sum(left * right, axis=(1, 2, 3, 4))


def local(
    rhs, log_perm, porosity, saturation, pressure, obs_values, obs_error, noise, well_cell, obs_well
):
    local_members, slab_x, plane_rows, plane_cols = log_perm.shape
    members = noise.shape[0]
    plane = plane_rows * plane_cols
    cells_dev = slab_x * plane
    slab_index = lax.axis_index("cell")
    slab_count = lax.axis_size("cell")
    stacked = jnp.stack([log_perm, saturation], axis=1)
    rimmed = with_halo(stacked, (("cell", 2),), 1)
    perm_pad = jnp.exp(rimmed[:, 0])
    sat_pad = rimmed[:, 1]
    trans_x, frac_x = face_pair(perm_pad[:, :-1], perm_pad[:, 1:], sat_pad[:, :-1], sat_pad[:, 1:])
    face_pos = lax.broadcasted_iota(jnp.int32, (slab_x + 1, 1, 1), 0)
    keep_face = jnp.where(
        face_pos == 0,
        slab_index > 0,
        jnp.where(face_pos == slab_x, slab_index < slab_count - 1, True),
    ).astype(jnp.float32)
    trans_x = trans_x * keep_face
    frac_x = frac_x * keep_face
    trans_y, frac_y, trans_z, frac_z = plane_faces(perm_pad[:, 1:-1], saturation)
    coeffs = (porosity / time_step, trans_x, frac_x, trans_y, frac_y, trans_z, frac_z)
    powers = [rhs]
    for jdx in range(KRYLOV):
        vector = powers[jdx]
        padded = with_halo(vector[:, 0], (("cell", 1),), 1)
        out_pressure, out_water = operator(padded, vector[:, 1], coeffs)
        image = jnp.stack([out_pressure, out_water], 1)
        powers.append(image - SHIFTS[jdx] * vector)
    entries = jnp.stack(
        [inner(powers[row], powers[col]) for row in range(KRYLOV + 1) for col in range(row + 1)], 0
    )
    entries = lax.psum(entries, "cell")
    solved = krylov_coefficients(entries)
    basis = powers
    increment = expand(solved[0]) * basis[0]
    for jdx in range(1, KRYLOV):
        increment = increment + expand(solved[jdx]) * basis[jdx]
    flat = jnp.stack([pressure + increment[:, 0], saturation + increment[:, 1]], 1).reshape(
        local_members, 2 * cells_dev
    )
    cells = jnp.take(well_cell, obs_well)
    wells = well_cell.shape[0]
    component = (jnp.arange(obs_well.shape[0], dtype=jnp.int32) >= wells).astype(jnp.int32)
    slab_row = cells // plane - slab_index * slab_x
    inside = (slab_row >= 0) & (slab_row < slab_x)
    local_cell = jnp.where(inside, slab_row * plane + cells % plane, 0)
    picked = jnp.take(flat, component * cells_dev + local_cell, axis=1) * inside.astype(jnp.float32)
    slab_pred = lax.psum(picked, "cell")
    predicted = lax.all_gather(slab_pred, "grp", axis=0, tiled=True)
    weights = ensemble_weights(predicted, obs_values, obs_error, noise)
    params = jnp.stack([log_perm, porosity], 1).reshape(local_members, 2 * cells_dev)
    offset = lax.axis_index("grp") * local_members
    scale_factor = 1.0 / math.sqrt(members - 1.0)
    scaled = params * scale_factor
    own_columns = lax.dynamic_slice_in_dim(weights, offset, local_members, 1)
    update = jnp.dot(
        own_columns.T,
        lax.all_gather(scaled, "grp", axis=0, tiled=True),
        precision=lax.Precision.HIGHEST,
        preferred_element_type=jnp.float32,
    )
    posterior = params + update
    posterior = posterior.reshape(local_members, 2, slab_x, plane_rows, plane_cols)
    return (increment, posterior[:, 0], posterior[:, 1])


def solution(mesh):
    in_specs = (
        P("grp", None, "cell", None, None),
        P("grp", "cell", None, None),
        P("grp", "cell", None, None),
        P("grp", "cell", None, None),
        P("grp", "cell", None, None),
        P(),
        P(),
        P(),
        P(),
        P(),
    )
    out_specs = (
        P("grp", None, "cell", None, None),
        P("grp", "cell", None, None),
        P("grp", "cell", None, None),
    )
    return jax.shard_map(local, mesh=mesh, in_specs=in_specs, out_specs=out_specs, check_vma=False)
```

```python
import functools
import math

import jax
import jax.numpy as jnp
from jax import lax
from jax.experimental import pallas as pl
from jax.experimental.pallas import tpu as pltpu
from jax.sharding import PartitionSpec as P

KRYLOV = 4
GROUPS = 4
SHIFTS = (1.5, 4.0, 8.0, 2.0)
MESH = pl.DeviceIdType.MESH

epsilon = 1e-06
time_step = 0.1
compress = 0.5
inflation = 4.0


def mobility(sat_field):
    return sat_field * sat_field + 0.5 * (1.0 - sat_field) * (1.0 - sat_field)


def face_pair(perm_low, perm_high, sat_low, sat_high):
    trans = (
        2.0
        * perm_low
        * perm_high
        / (perm_low + perm_high)
        * (0.5 * (mobility(sat_low) + mobility(sat_high)))
    )
    return (trans, trans * (0.5 * (sat_low + sat_high)))


def split3(value):
    high = value.astype(jnp.bfloat16)
    rest = value - high.astype(jnp.float32)
    middle = rest.astype(jnp.bfloat16)
    low = (rest - middle.astype(jnp.float32)).astype(jnp.bfloat16)
    return high, middle, low


def least_squares(columns, beta):
    rows = [list(column) for column in columns]
    cosines = []
    sines = []
    target = [beta] + [jnp.zeros_like(beta) for column in columns]
    for jdx in range(len(rows)):
        column = rows[jdx]
        for idx in range(jdx):
            upper = cosines[idx] * column[idx] + sines[idx] * column[idx + 1]
            column[idx + 1] = -sines[idx] * column[idx] + cosines[idx] * column[idx + 1]
            column[idx] = upper
        radius = jnp.sqrt(column[jdx] * column[jdx] + column[jdx + 1] * column[jdx + 1])
        cosines.append(column[jdx] / radius)
        sines.append(column[jdx + 1] / radius)
        column[jdx] = radius
        target[jdx + 1] = -sines[jdx] * target[jdx]
        target[jdx] = cosines[jdx] * target[jdx]
    count = len(rows)
    solved = [None] * count
    for jdx in reversed(range(count)):
        partial_sum = target[jdx]
        for idx in range(jdx + 1, count):
            partial_sum = partial_sum - rows[idx][jdx] * solved[idx]
        solved[jdx] = partial_sum / rows[jdx][jdx]
    return solved

def krylov_coefficients(entries):
    size = KRYLOV + 1
    zero = jnp.zeros_like(entries[0])

    def gram(row, col):
        row, col = max(row, col), min(row, col)
        return entries[row * (row + 1) // 2 + col]

    def times_gram(coef):
        out = []
        for row in range(size):
            total = zero
            for col, value in enumerate(coef):
                if value is not None:
                    total = total + gram(row, col) * value
            out.append(total)
        return out

    def dot(coef, image):
        total = zero
        for value, other in zip(coef, image):
            if value is not None:
                total = total + value * other
        return total

    beta = jnp.sqrt(gram(0, 0) + epsilon)
    basis = [[1.0 / beta] + [None] * KRYLOV]
    columns = []
    for jdx in range(KRYLOV):
        image = [None] * size
        for idx in range(jdx + 1):
            value = basis[jdx][idx]
            base = SHIFTS[idx] * value
            image[idx] = base if image[idx] is None else image[idx] + base
            image[idx + 1] = value
        mapped = times_gram(image)
        projected = [dot(basis[idx], mapped) for idx in range(jdx + 1)]
        for idx in range(jdx + 1):
            for pos in range(idx + 1):
                image[pos] = image[pos] - projected[idx] * basis[idx][pos]
        height = jnp.sqrt(jnp.maximum(dot(image, times_gram(image)), 0.0) + epsilon)
        columns.append(projected + [height])
        basis.append([None if value is None else value / height for value in image])
    solved = least_squares(columns, beta)
    mixed = []
    for pos in range(KRYLOV):
        total = zero
        for jdx in range(pos, KRYLOV):
            total = total + solved[jdx] * basis[jdx][pos]
        mixed.append(total)
    return mixed


def solve_kernel(
    cell_count, grp_count,
    rhs, lperm, poro, sat, pres, cells,
    inc_out, pred_out,
    powers, tx, gx, ty, gy, tz, gz, halo, gram, gslots, coefs, lhs, pslots, wslots,
    halo_send, halo_recv, gram_send, gram_recv, pick_send, pick_recv, pred_send, pred_recv,
):
    me = lax.axis_index("cell")
    mine = lax.axis_index("grp")
    members, _, slab, rows, cols = rhs.shape
    group = members // GROUPS
    has_prev, has_next = me > 0, me < cell_count - 1

    barrier = pltpu.get_barrier_semaphore()
    for step in range(1, cell_count):
        pl.semaphore_signal(
            barrier, inc=1, device_id={"cell": lax.rem(me + step, cell_count)}, device_id_type=MESH
        )
    for step in range(1, grp_count):
        pl.semaphore_signal(
            barrier, inc=1, device_id={"grp": lax.rem(mine + step, grp_count)}, device_id_type=MESH
        )
    pl.semaphore_wait(barrier, cell_count + grp_count - 2)

    def plane(field, part, at):
        part = pl.ds(part * group, group)
        if field == 0:
            return lperm.at[part, at]
        if field == 1:
            return sat.at[part, at]
        if field == 2:
            return rhs.at[part, 0, at]
        return powers.at[field - 3, part, 0, at]

    def halo_copy(field, part, side):
        return pltpu.make_async_remote_copy(
            src_ref=plane(field, part, slab - 1 if side == 0 else 0),
            dst_ref=halo.at[side, field, pl.ds(part * group, group)],
            send_sem=halo_send.at[side, field, part],
            recv_sem=halo_recv.at[side, field, part],
            device_id={"cell": (me + 1 if side == 0 else me + cell_count - 1) % cell_count},
            device_id_type=MESH,
        )

    def start_halo(field, part):
        @pl.when(has_next)
        def _():
            halo_copy(field, part, 0).start()

        @pl.when(has_prev)
        def _():
            halo_copy(field, part, 1).start()

    def wait_halo(field, part):
        @pl.when(has_prev)
        def _():
            halo_copy(field, part, 0).wait_recv()

        @pl.when(has_next)
        def _():
            halo_copy(field, part, 1).wait_recv()

    for part in range(GROUPS):
        for field in range(3):
            start_halo(field, part)

    @pl.when(me == 0)
    def _():
        halo[0] = jnp.zeros(halo.shape[1:], jnp.float32)

    @pl.when(me == cell_count - 1)
    def _():
        halo[1] = jnp.zeros(halo.shape[1:], jnp.float32)

    row_at = lax.broadcasted_iota(jnp.int32, (rows, cols), 0)
    col_at = lax.broadcasted_iota(jnp.int32, (rows, cols), 1)
    keep_rows = (row_at < rows - 1).astype(jnp.float32)
    keep_cols = (col_at < cols - 1).astype(jnp.float32)
    keep_low = has_prev.astype(jnp.float32)
    keep_high = has_next.astype(jnp.float32)

    def down(value, axis):
        return pltpu.roll(value, value.shape[axis] - 1, axis)

    def up(value, axis):
        return pltpu.roll(value, 1, axis)

    def inner_coeffs(m, carry):
        perm = [jnp.exp(lperm[m, x]) for x in range(slab)]
        water = [sat[m, x] for x in range(slab)]
        for x in range(slab):
            trans, frac = face_pair(perm[x], down(perm[x], 0), water[x], down(water[x], 0))
            ty[m, x] = trans * keep_rows
            gy[m, x] = frac * keep_rows
            trans, frac = face_pair(perm[x], down(perm[x], 1), water[x], down(water[x], 1))
            tz[m, x] = trans * keep_cols
            gz[m, x] = frac * keep_cols
            if x:
                trans, frac = face_pair(perm[x - 1], perm[x], water[x - 1], water[x])
                tx[m, x] = trans
                gx[m, x] = frac
        return carry

    lax.fori_loop(0, members, inner_coeffs, 0)

    def edge_coeffs(m):
        trans, frac = face_pair(jnp.exp(halo[0, 0, m]), jnp.exp(lperm[m, 0]), halo[0, 1, m], sat[m, 0])
        tx[m, 0] = trans * keep_low
        gx[m, 0] = frac * keep_low
        trans, frac = face_pair(
            jnp.exp(lperm[m, slab - 1]), jnp.exp(halo[1, 0, m]), sat[m, slab - 1], halo[1, 1, m]
        )
        tx[m, slab] = trans * keep_high
        gx[m, slab] = frac * keep_high

    def load(step, m, which, x):
        return rhs[m, which, x] if step == 0 else powers[step - 1, m, which, x]

    def apply(step, m):
        first = [halo[0, 2 + step, m]] + [load(step, m, 0, x) for x in range(slab)] + [halo[1, 2 + step, m]]
        flow_t, flow_g = [], []
        for x in range(slab + 1):
            diff = first[x + 1] - first[x]
            flow_t.append(tx[m, x] * diff)
            flow_g.append(gx[m, x] * diff)
        sums = [None] * (step + 2)
        start = None
        for x in range(slab):
            here = first[x + 1]
            second = load(step, m, 1, x)
            diff_y = down(here, 0) - here
            diff_z = down(here, 1) - here

            def net(flow_x, coef_y, coef_z):
                flow_y = coef_y * diff_y
                flow_z = coef_z * diff_z
                return (
                    flow_x[x] - flow_x[x + 1] + (up(flow_y, 0) - flow_y) + (up(flow_z, 1) - flow_z)
                )

            accum = poro[m, x] * (1.0 / time_step)
            out_u = accum * (compress * here + 0.5 * second) + net(flow_t, ty[m, x], tz[m, x])
            out_w = accum * second + net(flow_g, gy[m, x], gz[m, x])
            out_u = out_u - SHIFTS[step] * here
            out_w = out_w - SHIFTS[step] * second
            if step < KRYLOV - 1:
                powers[step, m, 0, x] = out_u
                powers[step, m, 1, x] = out_w
            for other in range(step + 2):
                if other == step + 1:
                    term = out_u * out_u + out_w * out_w
                elif other == step:
                    term = here * out_u + second * out_w
                else:
                    term = load(other, m, 0, x) * out_u + load(other, m, 1, x) * out_w
                sums[other] = term if x == 0 else sums[other] + term
            if step == 0:
                term = here * here + second * second
                start = term if x == 0 else start + term
        row = step + 1
        for other in range(step + 2):
            gram[row * (row + 1) // 2 + other, pl.ds(m, 1), :] = jnp.sum(
                sums[other], axis=0, keepdims=True
            )
        if step == 0:
            gram[0, pl.ds(m, 1), :] = jnp.sum(start, axis=0, keepdims=True)

    for step in range(KRYLOV):
        for part in range(GROUPS):
            if step == 0:
                wait_halo(0, part)
                wait_halo(1, part)
            wait_halo(2 + step, part)

            def body(m, carry):
                if step == 0:
                    edge_coeffs(m)
                apply(step, m)
                return carry

            lax.fori_loop(part * group, (part + 1) * group, body, 0)
            if step < KRYLOV - 1:
                start_halo(3 + step, part)

    def exchange(slots, here, count, axis, send, recv):
        copies = []
        for step in range(1, count):
            copies.append(
                pltpu.make_async_remote_copy(
                    src_ref=slots.at[here],
                    dst_ref=slots.at[here],
                    send_sem=send.at[step],
                    recv_sem=recv.at[step],
                    device_id={axis: lax.rem(here + step, count)},
                    device_id_type=MESH,
                )
            )
        for copy in copies:
            copy.start()
        for step in range(1, count):
            source = lax.rem(here + count - step, count)
            pltpu.make_async_remote_copy(
                src_ref=slots.at[source],
                dst_ref=slots.at[source],
                send_sem=send.at[step],
                recv_sem=recv.at[step],
                device_id={axis: lax.rem(here + step, count)},
                device_id_type=MESH,
            ).wait_recv()
        return copies

    pending = []
    count = (KRYLOV + 1) * (KRYLOV + 2) // 2
    lane = lax.broadcasted_iota(jnp.int32, (members, cols), 1)
    tile = jnp.zeros((members, cols), jnp.float32)
    for entry in range(count):
        tile = jnp.where(lane == entry, jnp.sum(gram[entry], axis=1, keepdims=True), tile)
    gslots[me] = tile
    pending += exchange(gslots, me, cell_count, "cell", gram_send, gram_recv)
    total = gslots[0]
    for slot in range(1, cell_count):
        total = total + gslots[slot]
    mixed = krylov_coefficients([total[:, entry : entry + 1] for entry in range(count)])
    for idx in range(KRYLOV):
        coefs[idx] = jnp.broadcast_to(mixed[idx], (members, cols))

    def combine(m, carry):
        scale = [coefs[idx, pl.ds(m, 1), :] for idx in range(KRYLOV)]
        for which in range(2):
            for x in range(slab):
                total = scale[0] * rhs[m, which, x]
                for idx in range(1, KRYLOV):
                    total = total + scale[idx] * powers[idx - 1, m, which, x]
                inc_out[m, which, x] = total
                state = (pres if which == 0 else sat)[m, x] + total
                at = pl.ds(pl.multiple_of(m * (slab * rows) + x * rows, rows), rows)
                for idx, piece in enumerate(split3(state)):
                    lhs[which, at, idx * cols : (idx + 1) * cols] = piece
        return carry

    lax.fori_loop(0, members, combine, 0)
    wells = cells.shape[1] // 2
    for which in range(2):
        cell = cells[:, which * wells : (which + 1) * wells]
        pick_col = lax.broadcasted_iota(jnp.int32, (cols, wells), 0) == lax.rem(cell, cols)
        pick_col = pick_col.astype(jnp.float32).astype(jnp.bfloat16)
        pick_row = (
            lax.broadcasted_iota(jnp.int32, (slab * rows, wells), 0) + me * (slab * rows)
            == lax.div(cell, cols)
        ).astype(jnp.float32)
        found = jnp.dot(
            lhs[which],
            jnp.concatenate([pick_col, pick_col, pick_col], axis=0),
            preferred_element_type=jnp.float32,
        )
        found = found.reshape(members, slab * rows, wells) * pick_row[None]
        pslots[me, :, which * wells : (which + 1) * wells] = jnp.sum(found, axis=1)
    pending += exchange(pslots, me, cell_count, "cell", pick_send, pick_recv)
    total = pslots[0]
    for slot in range(1, cell_count):
        total = total + pslots[slot]
    wslots[mine] = total
    pending += exchange(wslots, mine, grp_count, "grp", pred_send, pred_recv)
    pred_out[...] = wslots[...]
    for copy in pending:
        copy.wait_send()
    for field in range(2 + KRYLOV):
        for part in range(GROUPS):

            @pl.when(has_next)
            def _():
                halo_copy(field, part, 0).wait_send()

            @pl.when(has_prev)
            def _():
                halo_copy(field, part, 1).wait_send()


def dot3(left, right, dims):
    dot = functools.partial(
        lax.dot_general, dimension_numbers=(dims, ((), ())), preferred_element_type=jnp.float32
    )
    a = split3(left)
    b = split3(right)
    small = dot(a[0], b[2]) + dot(a[2], b[0]) + dot(a[1], b[1])
    return dot(a[0], b[0]) + (small + (dot(a[0], b[1]) + dot(a[1], b[0])))


def update_kernel(
    pred, obs, err, noise, all_perm, all_poro, own_perm, own_poro, perm_out, poro_out
):
    members = pred.shape[0]
    local_members = own_perm.shape[0]
    offset = lax.axis_index("grp") * local_members
    rows, cols = own_perm.shape[1:]
    sigma = math.sqrt(inflation) * err[...]
    predicted = pred[...]
    center = jnp.sum(predicted, axis=0, keepdims=True) * (1.0 / members)
    spread = (predicted - center) / (math.sqrt(members - 1.0) * sigma)
    innov = (obs[...] + sigma * noise[...] - predicted) / sigma
    row_at = lax.broadcasted_iota(jnp.int32, (members, members), 0)
    col_at = lax.broadcasted_iota(jnp.int32, (members, members), 1)
    gram = dot3(spread, spread, ((1,), (1,))) + (row_at == col_at).astype(jnp.float32)
    cross = dot3(spread, innov, ((1,), (1,)))
    both = jnp.concatenate([gram, cross], axis=1)
    line = lax.broadcasted_iota(jnp.int32, (members, 2 * members), 0)
    for k in range(members):
        pivot = both[k : k + 1, :] / both[k : k + 1, k : k + 1]
        factor = both[:, k : k + 1]
        both = jnp.where(line == k, pivot, both - factor * pivot)
    weights = both[:, members:]
    pick = (
        lax.broadcasted_iota(jnp.int32, (local_members, members), 0) + offset
        == lax.broadcasted_iota(jnp.int32, (local_members, members), 1)
    ).astype(jnp.float32)
    own = dot3(pick, weights, ((1,), (1,))) * (1.0 / math.sqrt(members - 1.0))
    high, middle, _ = split3(own)
    left = jnp.concatenate([high, middle, high], axis=1)
    for source, base, out in ((all_perm, own_perm, perm_out), (all_poro, own_poro, poro_out)):
        for row in range(0, rows, 2):
            block = jnp.concatenate([source[:, row, :], source[:, row + 1, :]], axis=1)
            top = block.astype(jnp.bfloat16)
            rest = (block - top.astype(jnp.float32)).astype(jnp.bfloat16)
            right = jnp.concatenate([top, top, rest], axis=0)
            update = jnp.dot(left, right, preferred_element_type=jnp.float32)
            out[:, row, :] = base[:, row, :] + update[:, :cols]
            out[:, row + 1, :] = base[:, row + 1, :] + update[:, cols:]


def local(
    rhs, log_perm, porosity, saturation, pressure, obs_values, obs_error, noise, well_cell, obs_well
):
    members, slab, rows, cols = log_perm.shape
    all_members, observations = noise.shape
    cell_count = lax.axis_size("cell")
    grp_count = lax.axis_size("grp")
    wells = well_cell.shape[0]
    hit = obs_well[:, None] == jnp.arange(wells, dtype=jnp.int32)[None, :]
    cells = jnp.sum(jnp.where(hit, well_cell[None, :], 0), axis=1, dtype=jnp.int32)[None, :]
    all_perm = lax.all_gather(log_perm, "grp", axis=0, tiled=True)
    all_poro = lax.all_gather(porosity, "grp", axis=0, tiled=True)
    vmem = pl.BlockSpec(memory_space=pltpu.VMEM)
    f32 = jnp.float32
    field = (members, slab, rows, cols)
    face = (members, slab + 1, rows, cols)
    entries = (KRYLOV + 1) * (KRYLOV + 2) // 2
    increment, predicted = pl.pallas_call(
        functools.partial(solve_kernel, cell_count, grp_count),
        out_shape=(
            jax.ShapeDtypeStruct(rhs.shape, f32),
            jax.ShapeDtypeStruct((grp_count, members, observations), f32),
        ),
        in_specs=[vmem] * 6,
        out_specs=(vmem, vmem),
        scratch_shapes=[
            pltpu.VMEM((KRYLOV - 1,) + rhs.shape, f32),
            pltpu.VMEM(face, f32),
            pltpu.VMEM(face, f32),
            pltpu.VMEM(field, f32),
            pltpu.VMEM(field, f32),
            pltpu.VMEM(field, f32),
            pltpu.VMEM(field, f32),
            pltpu.VMEM((2, 2 + KRYLOV, members, rows, cols), f32),
            pltpu.VMEM((entries, members, cols), f32),
            pltpu.VMEM((cell_count, members, cols), f32),
            pltpu.VMEM((KRYLOV, members, cols), f32),
            pltpu.VMEM((2, members * slab * rows, 3 * cols), jnp.bfloat16),
            pltpu.VMEM((cell_count, members, observations), f32),
            pltpu.VMEM((grp_count, members, observations), f32),
            pltpu.SemaphoreType.DMA((2, 2 + KRYLOV, GROUPS)),
            pltpu.SemaphoreType.DMA((2, 2 + KRYLOV, GROUPS)),
            pltpu.SemaphoreType.DMA((cell_count,)),
            pltpu.SemaphoreType.DMA((cell_count,)),
            pltpu.SemaphoreType.DMA((cell_count,)),
            pltpu.SemaphoreType.DMA((cell_count,)),
            pltpu.SemaphoreType.DMA((grp_count,)),
            pltpu.SemaphoreType.DMA((grp_count,)),
        ],
        compiler_params=pltpu.CompilerParams(
            collective_id=0, has_side_effects=True, vmem_limit_bytes=40 * 2**20
        ),
        cost_estimate=pl.CostEstimate(flops=10**8, bytes_accessed=10**8, transcendentals=0),
    )(rhs, log_perm, porosity, saturation, pressure, cells)
    flat = (members, slab * rows, cols)
    wide = (all_members, slab * rows, cols)
    perm_post, poro_post = pl.pallas_call(
        update_kernel,
        out_shape=(jax.ShapeDtypeStruct(flat, f32), jax.ShapeDtypeStruct(flat, f32)),
        in_specs=[vmem] * 8,
        out_specs=(vmem, vmem),
        compiler_params=pltpu.CompilerParams(vmem_limit_bytes=40 * 2**20),
    )(
        predicted.reshape(all_members, observations),
        obs_values[None, :],
        obs_error[None, :],
        noise,
        all_perm.reshape(wide),
        all_poro.reshape(wide),
        log_perm.reshape(flat),
        porosity.reshape(flat),
    )
    return (increment, perm_post.reshape(field), poro_post.reshape(field))


def solution(mesh):
    in_specs = (
        P("grp", None, "cell", None, None),
        P("grp", "cell", None, None),
        P("grp", "cell", None, None),
        P("grp", "cell", None, None),
        P("grp", "cell", None, None),
        P(),
        P(),
        P(),
        P(),
        P(),
    )
    out_specs = (
        P("grp", None, "cell", None, None),
        P("grp", "cell", None, None),
        P("grp", "cell", None, None),
    )
    return jax.shard_map(local, mesh=mesh, in_specs=in_specs, out_specs=out_specs, check_vma=False)
```

```python
import functools
import math

import jax
import jax.numpy as jnp
from jax import lax
from jax.experimental import pallas as pl
from jax.experimental.pallas import tpu as pltpu
from jax.sharding import PartitionSpec as P

KRYLOV = 4
GROUPS = 4
SHIFTS = (1.5, 4.0, 8.0, 2.0)
MESH = pl.DeviceIdType.MESH

epsilon = 1e-06
time_step = 0.1
compress = 0.5
inflation = 4.0


def mobility(sat_field):
    return sat_field * sat_field + 0.5 * (1.0 - sat_field) * (1.0 - sat_field)


def face_pair(perm_low, perm_high, sat_low, sat_high):
    trans = (
        2.0
        * perm_low
        * perm_high
        / (perm_low + perm_high)
        * (0.5 * (mobility(sat_low) + mobility(sat_high)))
    )
    return (trans, trans * (0.5 * (sat_low + sat_high)))


def split3(value):
    high = value.astype(jnp.bfloat16)
    rest = value - high.astype(jnp.float32)
    middle = rest.astype(jnp.bfloat16)
    low = (rest - middle.astype(jnp.float32)).astype(jnp.bfloat16)
    return high, middle, low


def least_squares(columns, beta):
    rows = [list(column) for column in columns]
    cosines = []
    sines = []
    target = [beta] + [jnp.zeros_like(beta) for column in columns]
    for jdx in range(len(rows)):
        column = rows[jdx]
        for idx in range(jdx):
            upper = cosines[idx] * column[idx] + sines[idx] * column[idx + 1]
            column[idx + 1] = -sines[idx] * column[idx] + cosines[idx] * column[idx + 1]
            column[idx] = upper
        radius = jnp.sqrt(column[jdx] * column[jdx] + column[jdx + 1] * column[jdx + 1])
        cosines.append(column[jdx] / radius)
        sines.append(column[jdx + 1] / radius)
        column[jdx] = radius
        target[jdx + 1] = -sines[jdx] * target[jdx]
        target[jdx] = cosines[jdx] * target[jdx]
    count = len(rows)
    solved = [None] * count
    for jdx in reversed(range(count)):
        partial_sum = target[jdx]
        for idx in range(jdx + 1, count):
            partial_sum = partial_sum - rows[idx][jdx] * solved[idx]
        solved[jdx] = partial_sum / rows[jdx][jdx]
    return solved

def krylov_coefficients(entries):
    size = KRYLOV + 1
    zero = jnp.zeros_like(entries[0])

    def gram(row, col):
        row, col = max(row, col), min(row, col)
        return entries[row * (row + 1) // 2 + col]

    def times_gram(coef):
        out = []
        for row in range(size):
            total = zero
            for col, value in enumerate(coef):
                if value is not None:
                    total = total + gram(row, col) * value
            out.append(total)
        return out

    def dot(coef, image):
        total = zero
        for value, other in zip(coef, image):
            if value is not None:
                total = total + value * other
        return total

    beta = jnp.sqrt(gram(0, 0) + epsilon)
    basis = [[1.0 / beta] + [None] * KRYLOV]
    columns = []
    for jdx in range(KRYLOV):
        image = [None] * size
        for idx in range(jdx + 1):
            value = basis[jdx][idx]
            base = SHIFTS[idx] * value
            image[idx] = base if image[idx] is None else image[idx] + base
            image[idx + 1] = value
        mapped = times_gram(image)
        projected = [dot(basis[idx], mapped) for idx in range(jdx + 1)]
        for idx in range(jdx + 1):
            for pos in range(idx + 1):
                image[pos] = image[pos] - projected[idx] * basis[idx][pos]
        height = jnp.sqrt(jnp.maximum(dot(image, times_gram(image)), 0.0) + epsilon)
        columns.append(projected + [height])
        basis.append([None if value is None else value / height for value in image])
    solved = least_squares(columns, beta)
    mixed = []
    for pos in range(KRYLOV):
        total = zero
        for jdx in range(pos, KRYLOV):
            total = total + solved[jdx] * basis[jdx][pos]
        mixed.append(total)
    return mixed


def solve_kernel(
    cell_count, grp_count,
    rhs_in, lperm_in, poro_in, sat_in, pres_in, cells,
    inc_hbm, pred_out, all_perm, all_poro,
    inc_out, inc_sem, rhs, lperm, poro, sat, pres, load_sem, par_send, par_recv,
    powers, tx, gx, ty, gy, tz, gz, halo, gram, gslots, coefs, lhs, pslots, wslots,
    halo_send, halo_recv, gram_send, gram_recv, pick_send, pick_recv, pred_send, pred_recv,
):
    me = lax.axis_index("cell")
    mine = lax.axis_index("grp")
    members, _, slab, rows, cols = rhs.shape
    group = members // GROUPS
    has_prev, has_next = me > 0, me < cell_count - 1

    loads = [
        pltpu.make_async_copy(source, target, load_sem.at[idx])
        for idx, (source, target) in enumerate(
            (
                (lperm_in, lperm),
                (sat_in, sat),
                (rhs_in, rhs),
                (poro_in, poro),
                (pres_in, pres),
                (lperm_in, all_perm.at[mine]),
                (poro_in, all_poro.at[mine]),
            )
        )
    ]
    for copy in loads:
        copy.start()

    barrier = pltpu.get_barrier_semaphore()
    for step in range(1, cell_count):
        pl.semaphore_signal(
            barrier, inc=1, device_id={"cell": lax.rem(me + step, cell_count)}, device_id_type=MESH
        )
    for step in range(1, grp_count):
        pl.semaphore_signal(
            barrier, inc=1, device_id={"grp": lax.rem(mine + step, grp_count)}, device_id_type=MESH
        )
    pl.semaphore_wait(barrier, cell_count + grp_count - 2)

    def plane(field, part, at):
        part = pl.ds(part * group, group)
        if field == 0:
            return lperm_in.at[part, at]
        if field == 1:
            return sat_in.at[part, at]
        if field == 2:
            return rhs_in.at[part, 0, at]
        return powers.at[field - 3, part, 0, at]

    def halo_copy(field, part, side):
        return pltpu.make_async_remote_copy(
            src_ref=plane(field, part, slab - 1 if side == 0 else 0),
            dst_ref=halo.at[side, field, pl.ds(part * group, group)],
            send_sem=halo_send.at[side, field, part],
            recv_sem=halo_recv.at[side, field, part],
            device_id={"cell": (me + 1 if side == 0 else me + cell_count - 1) % cell_count},
            device_id_type=MESH,
        )

    def start_halo(field, part):
        @pl.when(has_next)
        def _():
            halo_copy(field, part, 0).start()

        @pl.when(has_prev)
        def _():
            halo_copy(field, part, 1).start()

    def wait_halo(field, part):
        @pl.when(has_prev)
        def _():
            halo_copy(field, part, 0).wait_recv()

        @pl.when(has_next)
        def _():
            halo_copy(field, part, 1).wait_recv()

    for part in range(GROUPS):
        for field in range(3):
            start_halo(field, part)

    half = grp_count // 2
    sibling = mine + 1 - 2 * lax.rem(mine, 2)

    def param_copy(which, slot, target, at, relay):
        everyone = (all_perm, all_poro)[which]
        own = (lperm_in, poro_in)[which]
        return pltpu.make_async_remote_copy(
            src_ref=everyone.at[slot] if relay else own,
            dst_ref=everyone.at[slot],
            send_sem=par_send.at[which, at],
            recv_sem=par_recv.at[which, at],
            device_id={"grp": target},
            device_id_type=MESH,
        )

    params = []
    for which in range(2):
        for step in range(1, half):
            target = lax.rem(mine + 2 * step, grp_count)
            params.append(param_copy(which, mine, target, step, False))
        params.append(param_copy(which, mine, sibling, 0, False))
    for copy in params:
        copy.start()

    @pl.when(me == 0)
    def _():
        halo[0] = jnp.zeros(halo.shape[1:], jnp.float32)

    @pl.when(me == cell_count - 1)
    def _():
        halo[1] = jnp.zeros(halo.shape[1:], jnp.float32)

    row_at = lax.broadcasted_iota(jnp.int32, (rows, cols), 0)
    col_at = lax.broadcasted_iota(jnp.int32, (rows, cols), 1)
    keep_rows = (row_at < rows - 1).astype(jnp.float32)
    keep_cols = (col_at < cols - 1).astype(jnp.float32)
    keep_low = has_prev.astype(jnp.float32)
    keep_high = has_next.astype(jnp.float32)

    def down(value, axis):
        return pltpu.roll(value, value.shape[axis] - 1, axis)

    def up(value, axis):
        return pltpu.roll(value, 1, axis)

    def inner_coeffs(m, carry):
        perm = [jnp.exp(lperm[m, x]) for x in range(slab)]
        water = [sat[m, x] for x in range(slab)]
        for x in range(slab):
            trans, frac = face_pair(perm[x], down(perm[x], 0), water[x], down(water[x], 0))
            ty[m, x] = trans * keep_rows
            gy[m, x] = frac * keep_rows
            trans, frac = face_pair(perm[x], down(perm[x], 1), water[x], down(water[x], 1))
            tz[m, x] = trans * keep_cols
            gz[m, x] = frac * keep_cols
            if x:
                trans, frac = face_pair(perm[x - 1], perm[x], water[x - 1], water[x])
                tx[m, x] = trans
                gx[m, x] = frac
        return carry

    loads[0].wait()
    loads[1].wait()
    lax.fori_loop(0, members, inner_coeffs, 0)
    for copy in loads[2:]:
        copy.wait()

    def edge_coeffs(m):
        trans, frac = face_pair(jnp.exp(halo[0, 0, m]), jnp.exp(lperm[m, 0]), halo[0, 1, m], sat[m, 0])
        tx[m, 0] = trans * keep_low
        gx[m, 0] = frac * keep_low
        trans, frac = face_pair(
            jnp.exp(lperm[m, slab - 1]), jnp.exp(halo[1, 0, m]), sat[m, slab - 1], halo[1, 1, m]
        )
        tx[m, slab] = trans * keep_high
        gx[m, slab] = frac * keep_high

    def load(step, m, which, x):
        return rhs[m, which, x] if step == 0 else powers[step - 1, m, which, x]

    def apply(step, m):
        first = [halo[0, 2 + step, m]] + [load(step, m, 0, x) for x in range(slab)] + [halo[1, 2 + step, m]]
        flow_t, flow_g = [], []
        for x in range(slab + 1):
            diff = first[x + 1] - first[x]
            flow_t.append(tx[m, x] * diff)
            flow_g.append(gx[m, x] * diff)
        sums = [None] * (step + 2)
        start = None
        for x in range(slab):
            here = first[x + 1]
            second = load(step, m, 1, x)
            diff_y = down(here, 0) - here
            diff_z = down(here, 1) - here

            def net(flow_x, coef_y, coef_z):
                flow_y = coef_y * diff_y
                flow_z = coef_z * diff_z
                return (
                    flow_x[x] - flow_x[x + 1] + (up(flow_y, 0) - flow_y) + (up(flow_z, 1) - flow_z)
                )

            accum = poro[m, x] * (1.0 / time_step)
            out_u = accum * (compress * here + 0.5 * second) + net(flow_t, ty[m, x], tz[m, x])
            out_w = accum * second + net(flow_g, gy[m, x], gz[m, x])
            out_u = out_u - SHIFTS[step] * here
            out_w = out_w - SHIFTS[step] * second
            if step < KRYLOV - 1:
                powers[step, m, 0, x] = out_u
                powers[step, m, 1, x] = out_w
            for other in range(step + 2):
                if other == step + 1:
                    term = out_u * out_u + out_w * out_w
                elif other == step:
                    term = here * out_u + second * out_w
                else:
                    term = load(other, m, 0, x) * out_u + load(other, m, 1, x) * out_w
                sums[other] = term if x == 0 else sums[other] + term
            if step == 0:
                term = here * here + second * second
                start = term if x == 0 else start + term
        row = step + 1
        for other in range(step + 2):
            gram[row * (row + 1) // 2 + other, pl.ds(m, 1), :] = jnp.sum(
                sums[other], axis=0, keepdims=True
            )
        if step == 0:
            gram[0, pl.ds(m, 1), :] = jnp.sum(start, axis=0, keepdims=True)

    for step in range(KRYLOV):
        for part in range(GROUPS):
            if step == 0:
                wait_halo(0, part)
                wait_halo(1, part)
            wait_halo(2 + step, part)

            def body(m, carry):
                if step == 0:
                    edge_coeffs(m)
                apply(step, m)
                return carry

            lax.fori_loop(part * group, (part + 1) * group, body, 0)
            if step < KRYLOV - 1:
                start_halo(3 + step, part)

    def exchange(slots, here, count, axis, send, recv):
        copies = []
        for step in range(1, count):
            copies.append(
                pltpu.make_async_remote_copy(
                    src_ref=slots.at[here],
                    dst_ref=slots.at[here],
                    send_sem=send.at[step],
                    recv_sem=recv.at[step],
                    device_id={axis: lax.rem(here + step, count)},
                    device_id_type=MESH,
                )
            )
        for copy in copies:
            copy.start()
        for step in range(1, count):
            source = lax.rem(here + count - step, count)
            pltpu.make_async_remote_copy(
                src_ref=slots.at[source],
                dst_ref=slots.at[source],
                send_sem=send.at[step],
                recv_sem=recv.at[step],
                device_id={axis: lax.rem(here + step, count)},
                device_id_type=MESH,
            ).wait_recv()
        return copies

    pending = []
    count = (KRYLOV + 1) * (KRYLOV + 2) // 2
    lane = lax.broadcasted_iota(jnp.int32, (members, cols), 1)
    tile = jnp.zeros((members, cols), jnp.float32)
    for entry in range(count):
        tile = jnp.where(lane == entry, jnp.sum(gram[entry], axis=1, keepdims=True), tile)
    gslots[me] = tile
    pending += exchange(gslots, me, cell_count, "cell", gram_send, gram_recv)
    total = gslots[0]
    for slot in range(1, cell_count):
        total = total + gslots[slot]
    mixed = krylov_coefficients([total[:, entry : entry + 1] for entry in range(count)])
    for idx in range(KRYLOV):
        coefs[idx] = jnp.broadcast_to(mixed[idx], (members, cols))
    for which in range(2):
        for step in range(1, half):
            source = lax.rem(mine + grp_count - 2 * step, grp_count)
            param_copy(which, source, sibling, step, True).wait_recv()
            copy = param_copy(which, source, sibling, half - 1 + step, True)
            copy.start()
            params.append(copy)

    def combine(m, carry):
        scale = [coefs[idx, pl.ds(m, 1), :] for idx in range(KRYLOV)]
        for which in range(2):
            for x in range(slab):
                total = scale[0] * rhs[m, which, x]
                for idx in range(1, KRYLOV):
                    total = total + scale[idx] * powers[idx - 1, m, which, x]
                inc_out[m, which, x] = total
                state = (pres if which == 0 else sat)[m, x] + total
                at = pl.ds(pl.multiple_of(m * (slab * rows) + x * rows, rows), rows)
                for idx, piece in enumerate(split3(state)):
                    lhs[which, at, idx * cols : (idx + 1) * cols] = piece
        return carry

    lax.fori_loop(0, members, combine, 0)
    store = pltpu.make_async_copy(inc_out, inc_hbm, inc_sem)
    store.start()
    wells = cells.shape[1] // 2
    for which in range(2):
        cell = cells[:, which * wells : (which + 1) * wells]
        pick_col = lax.broadcasted_iota(jnp.int32, (cols, wells), 0) == lax.rem(cell, cols)
        pick_col = pick_col.astype(jnp.float32).astype(jnp.bfloat16)
        pick_row = (
            lax.broadcasted_iota(jnp.int32, (slab * rows, wells), 0) + me * (slab * rows)
            == lax.div(cell, cols)
        ).astype(jnp.float32)
        found = jnp.dot(
            lhs[which],
            jnp.concatenate([pick_col, pick_col, pick_col], axis=0),
            preferred_element_type=jnp.float32,
        )
        found = found.reshape(members, slab * rows, wells) * pick_row[None]
        pslots[me, :, which * wells : (which + 1) * wells] = jnp.sum(found, axis=1)
    pending += exchange(pslots, me, cell_count, "cell", pick_send, pick_recv)
    total = pslots[0]
    for slot in range(1, cell_count):
        total = total + pslots[slot]
    wslots[mine] = total
    pending += exchange(wslots, mine, grp_count, "grp", pred_send, pred_recv)
    pred_out[...] = wslots[...]
    for which in range(2):
        param_copy(which, sibling, sibling, 0, True).wait_recv()
        for step in range(1, half):
            source = lax.rem(sibling + grp_count - 2 * step, grp_count)
            param_copy(which, source, sibling, half - 1 + step, True).wait_recv()
    for copy in pending + params:
        copy.wait_send()
    store.wait()
    for field in range(2 + KRYLOV):
        for part in range(GROUPS):

            @pl.when(has_next)
            def _():
                halo_copy(field, part, 0).wait_send()

            @pl.when(has_prev)
            def _():
                halo_copy(field, part, 1).wait_send()


def dot3(left, right, dims):
    dot = functools.partial(
        lax.dot_general, dimension_numbers=(dims, ((), ())), preferred_element_type=jnp.float32
    )
    a = split3(left)
    b = split3(right)
    small = dot(a[0], b[2]) + dot(a[2], b[0]) + dot(a[1], b[1])
    return dot(a[0], b[0]) + (small + (dot(a[0], b[1]) + dot(a[1], b[0])))


def update_kernel(
    pred, obs, err, noise, perm_in, poro_in, own_perm_in, own_poro_in, inc,
    perm_out, poro_out, inc_out,
    all_perm, all_poro, own_perm, own_poro, sems,
):
    copies = [
        pltpu.make_async_copy(source, target, sems.at[idx])
        for idx, (source, target) in enumerate(
            (
                (perm_in, all_perm),
                (poro_in, all_poro),
                (own_perm_in, own_perm),
                (own_poro_in, own_poro),
                (inc, inc_out),
            )
        )
    ]
    for copy in copies:
        copy.start()
    members = pred.shape[0]
    local_members = own_perm_in.shape[0]
    offset = lax.axis_index("grp") * local_members
    rows, cols = own_perm_in.shape[1:]
    sigma = math.sqrt(inflation) * err[...]
    predicted = pred[...]
    center = jnp.sum(predicted, axis=0, keepdims=True) * (1.0 / members)
    spread = (predicted - center) / (math.sqrt(members - 1.0) * sigma)
    innov = (obs[...] + sigma * noise[...] - predicted) / sigma
    row_at = lax.broadcasted_iota(jnp.int32, (members, members), 0)
    col_at = lax.broadcasted_iota(jnp.int32, (members, members), 1)
    gram = dot3(spread, spread, ((1,), (1,))) + (row_at == col_at).astype(jnp.float32)
    cross = dot3(spread, innov, ((1,), (1,)))
    both = jnp.concatenate([gram, cross], axis=1)
    line = lax.broadcasted_iota(jnp.int32, (members, 2 * members), 0)
    for k in range(members):
        pivot = both[k : k + 1, :] / both[k : k + 1, k : k + 1]
        factor = both[:, k : k + 1]
        both = jnp.where(line == k, pivot, both - factor * pivot)
    weights = both[:, members:]
    pick = (
        lax.broadcasted_iota(jnp.int32, (local_members, members), 0) + offset
        == lax.broadcasted_iota(jnp.int32, (local_members, members), 1)
    ).astype(jnp.float32)
    own = dot3(pick, weights, ((1,), (1,))) * (1.0 / math.sqrt(members - 1.0))
    high, middle, _ = split3(own)
    left = jnp.concatenate([high, middle, high], axis=1)
    for copy in copies[:4]:
        copy.wait()
    for source, base, out in ((all_perm, own_perm, perm_out), (all_poro, own_poro, poro_out)):
        for row in range(0, rows, 2):
            block = jnp.concatenate([source[:, row, :], source[:, row + 1, :]], axis=1)
            top = block.astype(jnp.bfloat16)
            rest = (block - top.astype(jnp.float32)).astype(jnp.bfloat16)
            right = jnp.concatenate([top, top, rest], axis=0)
            update = jnp.dot(left, right, preferred_element_type=jnp.float32)
            out[:, row, :] = base[:, row, :] + update[:, :cols]
            out[:, row + 1, :] = base[:, row + 1, :] + update[:, cols:]
    copies[4].wait()


def local(
    rhs, log_perm, porosity, saturation, pressure, obs_values, obs_error, noise, well_cell, obs_well
):
    members, slab, rows, cols = log_perm.shape
    all_members, observations = noise.shape
    cell_count = lax.axis_size("cell")
    grp_count = lax.axis_size("grp")
    wells = well_cell.shape[0]
    hit = obs_well[:, None] == jnp.arange(wells, dtype=jnp.int32)[None, :]
    cells = jnp.sum(jnp.where(hit, well_cell[None, :], 0), axis=1, dtype=jnp.int32)[None, :]
    vmem = pl.BlockSpec(memory_space=pltpu.VMEM)
    f32 = jnp.float32
    field = (members, slab, rows, cols)
    face = (members, slab + 1, rows, cols)
    entries = (KRYLOV + 1) * (KRYLOV + 2) // 2
    hbm = pl.BlockSpec(memory_space=pltpu.HBM)
    increment, predicted, all_perm, all_poro = pl.pallas_call(
        functools.partial(solve_kernel, cell_count, grp_count),
        out_shape=(
            jax.ShapeDtypeStruct(rhs.shape, f32),
            jax.ShapeDtypeStruct((grp_count, members, observations), f32),
            jax.ShapeDtypeStruct((grp_count,) + field, f32),
            jax.ShapeDtypeStruct((grp_count,) + field, f32),
        ),
        in_specs=[hbm] * 5 + [vmem],
        out_specs=(hbm, vmem, hbm, hbm),
        scratch_shapes=[
            pltpu.VMEM(rhs.shape, f32),
            pltpu.SemaphoreType.DMA,
            pltpu.VMEM(rhs.shape, f32),
            pltpu.VMEM(field, f32),
            pltpu.VMEM(field, f32),
            pltpu.VMEM(field, f32),
            pltpu.VMEM(field, f32),
            pltpu.SemaphoreType.DMA((7,)),
            pltpu.SemaphoreType.DMA((2, grp_count - 1)),
            pltpu.SemaphoreType.DMA((2, grp_count - 1)),
            pltpu.VMEM((KRYLOV - 1,) + rhs.shape, f32),
            pltpu.VMEM(face, f32),
            pltpu.VMEM(face, f32),
            pltpu.VMEM(field, f32),
            pltpu.VMEM(field, f32),
            pltpu.VMEM(field, f32),
            pltpu.VMEM(field, f32),
            pltpu.VMEM((2, 2 + KRYLOV, members, rows, cols), f32),
            pltpu.VMEM((entries, members, cols), f32),
            pltpu.VMEM((cell_count, members, cols), f32),
            pltpu.VMEM((KRYLOV, members, cols), f32),
            pltpu.VMEM((2, members * slab * rows, 3 * cols), jnp.bfloat16),
            pltpu.VMEM((cell_count, members, observations), f32),
            pltpu.VMEM((grp_count, members, observations), f32),
            pltpu.SemaphoreType.DMA((2, 2 + KRYLOV, GROUPS)),
            pltpu.SemaphoreType.DMA((2, 2 + KRYLOV, GROUPS)),
            pltpu.SemaphoreType.DMA((cell_count,)),
            pltpu.SemaphoreType.DMA((cell_count,)),
            pltpu.SemaphoreType.DMA((cell_count,)),
            pltpu.SemaphoreType.DMA((cell_count,)),
            pltpu.SemaphoreType.DMA((grp_count,)),
            pltpu.SemaphoreType.DMA((grp_count,)),
        ],
        compiler_params=pltpu.CompilerParams(
            collective_id=0, has_side_effects=True, vmem_limit_bytes=58 * 2**20
        ),
        cost_estimate=pl.CostEstimate(flops=10**8, bytes_accessed=10**8, transcendentals=0),
    )(rhs, log_perm, porosity, saturation, pressure, cells)
    flat = (members, slab * rows, cols)
    wide = (all_members, slab * rows, cols)
    perm_post, poro_post, increment = pl.pallas_call(
        update_kernel,
        out_shape=(
            jax.ShapeDtypeStruct(flat, f32),
            jax.ShapeDtypeStruct(flat, f32),
            jax.ShapeDtypeStruct(rhs.shape, f32),
        ),
        in_specs=[vmem] * 4 + [hbm] * 5,
        out_specs=(vmem, vmem, hbm),
        scratch_shapes=[
            pltpu.VMEM(wide, f32),
            pltpu.VMEM(wide, f32),
            pltpu.VMEM(flat, f32),
            pltpu.VMEM(flat, f32),
            pltpu.SemaphoreType.DMA((5,)),
        ],
        compiler_params=pltpu.CompilerParams(vmem_limit_bytes=60 * 2**20),
    )(
        predicted.reshape(all_members, observations),
        obs_values[None, :],
        obs_error[None, :],
        noise,
        all_perm.reshape(wide),
        all_poro.reshape(wide),
        log_perm.reshape(flat),
        porosity.reshape(flat),
        increment,
    )
    return (increment, perm_post.reshape(field), poro_post.reshape(field))


def solution(mesh):
    in_specs = (
        P("grp", None, "cell", None, None),
        P("grp", "cell", None, None),
        P("grp", "cell", None, None),
        P("grp", "cell", None, None),
        P("grp", "cell", None, None),
        P(),
        P(),
        P(),
        P(),
        P(),
    )
    out_specs = (
        P("grp", None, "cell", None, None),
        P("grp", "cell", None, None),
        P("grp", "cell", None, None),
    )
    return jax.shard_map(local, mesh=mesh, in_specs=in_specs, out_specs=out_specs, check_vma=False)
```
